512 devices in a mesh: row: 16 (over y, core), col: 32 (over x, z).
Axes of the slice: x: 4, y: 8, z: 8, core: 2. Of those that a mesh axis runs over, the one named last changes fastest.
Arguments:
- matrix: bfloat16 [8192, 131072], P('row', 'col'), may hold values from -6 to 6
- sketch: bfloat16 [131072, 128], P('col'), may hold values from -0.015625 to 0.015625
Outputs:
- basis: bfloat16 [8192, 128], P('row')
- projected: bfloat16 [128, 131072], P(None, 'col')
The draws below stay inside these ranges and needn't reach their ends.
All inputs are finite; a program needn't handle non-finite values.
Results may differ from the reference program's by a relative error of at most 0.0048.
Values may be sent and summed in bfloat16 or wider, within the bound.
No kernel may reach another device: no remote copies, remote signals or barrier semaphores. Data moves between devices by JAX's collectives and lax.ppermute only.
A program may use at most 64 MiB of HBM per device.

```python
import jax
import jax.numpy as jnp
from jax import lax

C_DEV = 4096
K = 128
ROWS = 8192
COLS = 131072
N_COL = 32


def shard_levels(key, dims, shards, least, top_value):
    def one(position, blocks):
        heights = jax.random.uniform(jax.random.fold_in(jax.random.fold_in(key, 6), position), (blocks,), jnp.float32, least / len(shards), top_value / len(shards))
        return jnp.repeat(jnp.exp(heights), dims[position] // blocks).reshape((-1,) + (1,) * (len(dims) - position - 1))

    gain = one(*shards[0])
    for cut in shards[1:]:
        gain = gain * one(*cut)
    return gain


def bell_draw(stream_key, dims, width, reach, split=(), dtype=jnp.bfloat16):
    loudness = shard_levels(stream_key, dims, split, -0.22, 0.18) if split else 1.0
    array = jax.random.normal(stream_key, dims, jnp.float32) * width * loudness
    return jnp.minimum(jnp.maximum(array, -reach), reach).astype(dtype)


def setup_inputs(seed: int = 0) -> dict:
    keys = jax.random.split(jax.random.key(seed), 3)
    return {
        "matrix": bell_draw(keys[0], (ROWS, COLS), 1.0, 6.0, ((0, 16), (1, 32))),
        "sketch": bell_draw(keys[1], (COLS, K), COLS ** -0.5, 0.015625, ((0, 32),)),
    }


def reference(matrix, sketch):

    def add_block(j, total):
        tile = lax.dynamic_slice_in_dim(matrix, j * C_DEV, C_DEV, 1).astype(jnp.float32)
        omega = lax.dynamic_slice_in_dim(sketch, j * C_DEV, C_DEV, 0).astype(jnp.float32)
        return total + jnp.dot(tile, omega, precision=lax.Precision.HIGHEST)
    sampled = lax.fori_loop(0, N_COL, add_block, jnp.zeros((ROWS, K), jnp.float32))
    gram = jnp.dot(sampled.T, sampled, precision=lax.Precision.HIGHEST)
    lower = jnp.linalg.cholesky(gram)
    solved = lax.linalg.triangular_solve(lower, sampled, left_side=False, lower=True, transpose_a=True)
    basis = solved.astype(jnp.bfloat16)
    basis_wide = basis.astype(jnp.float32)

    def project_block(j):
        tile = lax.dynamic_slice_in_dim(matrix, j * C_DEV, C_DEV, 1).astype(jnp.float32)
        return jnp.dot(basis_wide.T, tile, precision=lax.Precision.HIGHEST)
    pieces = lax.map(project_block, jnp.arange(N_COL))
    projected = jnp.transpose(pieces, (1, 0, 2)).reshape(K, COLS).astype(jnp.bfloat16)
    return (basis, projected)
```

```python
import jax
import jax.numpy as jnp
from jax import lax
from jax.experimental import pallas as pl
from jax.experimental.pallas import tpu as pltpu
from jax.sharding import PartitionSpec as P

K = 128
T = 8
NP = K // T
NX, NY, NZ = 4, 8, 8
NROW, NCOL = 16, 32
F32 = jnp.float32
BF16 = jnp.bfloat16
HIGH = lax.Precision.HIGHEST


def sub_row(x, i):
    return jnp.broadcast_to(x[i : i + 1, :], (T, K))


def lane_col(x, i):
    return jnp.broadcast_to(x[:, i : i + 1], (T, K))


def chol_inv_kernel(g_ref, o_ref):
    sub = lax.broadcasted_iota(jnp.int32, (T, K), 0)
    lane = lax.broadcasted_iota(jnp.int32, (T, K), 1)
    a = [g_ref[p * T : (p + 1) * T, :] for p in range(NP)]
    for k in range(NP):
        lo = k * T
        inside = (lane >= lo) & (lane < lo + T)
        c = [lane_col(a[k], lo + j) for j in range(T)]
        x = jnp.where(inside, jnp.where(lane - lo == sub, 1.0, 0.0), a[k])
        u = x
        dvec = c[0]
        for j in range(T):
            at = sub == j
            d = sub_row(c[j], j)
            r = 1.0 / d
            u = jnp.where(at, x, u)
            dvec = jnp.where(at, d, dvec)
            xj = sub_row(x, j)
            cj = c[j]
            x = jnp.where(at, xj * r, x - (cj * xj) * r)
            for l in range(j + 1, T):
                cl = sub_row(c[l], j)
                c[l] = jnp.where(at, cl * r, c[l] - (cj * cl) * r)
        rows = [sub_row(x, j) for j in range(T)]
        for p in range(k + 1, NP):
            terms = [lane_col(a[p], lo + j) * rows[j] for j in range(T)]
            while len(terms) > 1:
                terms = [terms[i] + terms[i + 1] for i in range(0, len(terms), 2)]
            a[p] = jnp.where(inside, 0.0, a[p]) - terms[0]
        o_ref[lo : lo + T, :] = jnp.where(lane <= lo + sub, u * lax.rsqrt(dvec), 0.0)


def chol_inv(gram):
    return pl.pallas_call(
        chol_inv_kernel,
        out_shape=jax.ShapeDtypeStruct((K, K), F32),
        name="chol_inv",
    )(gram)


def w_kernel(core_ref, s_ref, m_ref, own_ref, other_ref):
    turned = s_ref[...].T
    high = turned.astype(BF16)
    low = (turned - high.astype(F32)).astype(BF16)
    hl = jnp.concatenate([high, low], axis=0)
    width = own_ref.shape[2]
    core = core_ref[0]
    for half, out_ref in ((1 - core, other_ref), (core, own_ref)):
        for y in range(NY):
            at = pl.multiple_of((half * NY + y) * width, width)
            w = jnp.dot(hl, m_ref[:, pl.ds(at, width)], preferred_element_type=F32)
            out_ref[y] = w[:K] + w[K:]


def sketch_rows(sampled, matrix, core):
    width = matrix.shape[1] // NROW
    vmem = pl.BlockSpec(memory_space=pltpu.VMEM)
    return pl.pallas_call(
        w_kernel,
        in_specs=[pl.BlockSpec(memory_space=pltpu.SMEM), vmem, vmem],
        out_specs=[vmem, vmem],
        out_shape=[jax.ShapeDtypeStruct((NY, K, width), F32)] * 2,
        cost_estimate=pl.CostEstimate(
            flops=4 * K * matrix.size, bytes_accessed=9 << 20, transcendentals=0
        ),
        compiler_params=pltpu.CompilerParams(vmem_limit_bytes=40 << 20),
        name="sketch_rows",
    )(core.astype(jnp.int32).reshape(1), sampled, matrix)


def finish_kernel(inv_ref, parts_ref, out_ref):
    total = parts_ref[0]
    for k in range(1, NY):
        total = total + parts_ref[k]
    piece = jnp.dot(inv_ref[...], total, precision=HIGH, preferred_element_type=F32).astype(BF16)
    for k in range(NY):
        out_ref[k] = piece


def finish(inverse, parts):
    return pl.pallas_call(
        finish_kernel,
        out_shape=jax.ShapeDtypeStruct(parts.shape, BF16),
        name="finish",
    )(inverse, parts)


def place_kernel(core_ref, own_ref, other_ref, out_ref):
    width = own_ref.shape[2]
    core = core_ref[0]
    for half, ref in ((core, own_ref), (1 - core, other_ref)):
        for y in range(NY):
            at = pl.multiple_of((half * NY + y) * width, width)
            out_ref[:, pl.ds(at, width)] = ref[y]


def place(own, other, core):
    vmem = pl.BlockSpec(memory_space=pltpu.VMEM)
    return pl.pallas_call(
        place_kernel,
        in_specs=[pl.BlockSpec(memory_space=pltpu.SMEM), vmem, vmem],
        out_specs=vmem,
        out_shape=jax.ShapeDtypeStruct((K, NROW * own.shape[2]), BF16),
        name="place",
    )(core.astype(jnp.int32).reshape(1), own, other)


SWAP = [(i, i ^ 1) for i in range(NROW)]
Y_GROUPS = [[2 * k + core for k in range(NY)] for core in range(2)]
Z_GROUPS = [[x * NZ + k for k in range(NZ)] for x in range(NX)]


def spread(block, n):
    return jnp.broadcast_to(block[None], (n, *block.shape))


def local(matrix, sketch):
    core = lax.axis_index("row") % 2
    z = lax.axis_index("col") % NZ
    rows = matrix.shape[0]

    partial_value = jnp.dot(matrix, sketch, preferred_element_type=F32)
    parts = lax.all_to_all(partial_value.reshape(NCOL, rows // NCOL, K), "col", 0, 0)
    share = jnp.sum(parts, axis=0)
    sampled = lax.all_to_all(spread(share, NCOL), "col", 0, 0).reshape(rows, K)

    gram = jnp.dot(sampled.T, sampled, precision=HIGH)
    strip = lax.dynamic_slice_in_dim(gram, z * (K // NZ), K // NZ, 0)
    strip = jnp.sum(lax.all_to_all(spread(strip, NROW), "row", 0, 0), axis=0)
    gram = lax.all_to_all(spread(strip, NZ), "col", 0, 0, axis_index_groups=Z_GROUPS)
    inverse = chol_inv(gram.reshape(K, K))

    own, other = sketch_rows(sampled, matrix, core)
    mine = own + lax.ppermute(other, "row", SWAP)
    parts = lax.all_to_all(mine, "row", 0, 0, axis_index_groups=Y_GROUPS)

    pieces = lax.all_to_all(finish(inverse, parts), "row", 0, 0, axis_index_groups=Y_GROUPS)
    basis = lax.dot_general(sampled, inverse, (((1,), (1,)), ((), ())), precision=HIGH).astype(BF16)
    return basis, place(pieces, lax.ppermute(pieces, "row", SWAP), core)


def solution(mesh):
    return jax.shard_map(
        local,
        mesh=mesh,
        in_specs=(P("row", "col"), P("col", None)),
        out_specs=(P("row", None), P(None, "col")),
        check_vma=False,
    )
```

```python
import jax
import jax.numpy as jnp
from jax import lax
from jax.experimental import pallas as pl
from jax.experimental.pallas import tpu as pltpu
from jax.sharding import PartitionSpec as P

K = 128
T = 8
NP = K // T
NX, NY, NZ = 4, 8, 8
NROW, NCOL = 16, 32
F32 = jnp.float32
BF16 = jnp.bfloat16
HIGH = lax.Precision.HIGHEST


def room(mib):
    return pltpu.CompilerParams(vmem_limit_bytes=mib << 20)


def sub_row(x, i):
    return jnp.broadcast_to(x[i : i + 1, :], (T, K))


def lane_col(x, i):
    return jnp.broadcast_to(x[:, i : i + 1], (T, K))


def chol_inv_kernel(g_ref, o_ref):
    sub = lax.broadcasted_iota(jnp.int32, (T, K), 0)
    lane = lax.broadcasted_iota(jnp.int32, (T, K), 1)
    a = [g_ref[p * T : (p + 1) * T, :] for p in range(NP)]
    for k in range(NP):
        lo = k * T
        inside = (lane >= lo) & (lane < lo + T)
        c = [lane_col(a[k], lo + j) for j in range(T)]
        x = jnp.where(inside, jnp.where(lane - lo == sub, 1.0, 0.0), a[k])
        u = x
        dvec = c[0]
        for j in range(T):
            at = sub == j
            d = sub_row(c[j], j)
            r = 1.0 / d
            u = jnp.where(at, x, u)
            dvec = jnp.where(at, d, dvec)
            xj = sub_row(x, j)
            cj = c[j]
            x = jnp.where(at, xj * r, x - (cj * xj) * r)
            for l in range(j + 1, T):
                cl = sub_row(c[l], j)
                c[l] = jnp.where(at, cl * r, c[l] - (cj * cl) * r)
        rows = [sub_row(x, j) for j in range(T)]
        for p in range(k + 1, NP):
            terms = [lane_col(a[p], lo + j) * rows[j] for j in range(T)]
            while len(terms) > 1:
                terms = [terms[i] + terms[i + 1] for i in range(0, len(terms), 2)]
            a[p] = jnp.where(inside, 0.0, a[p]) - terms[0]
        o_ref[lo : lo + T, :] = jnp.where(lane <= lo + sub, u * lax.rsqrt(dvec), 0.0)


def chol_inv(gram):
    return pl.pallas_call(
        chol_inv_kernel,
        out_shape=jax.ShapeDtypeStruct((K, K), F32),
        compiler_params=room(4),
        name="chol_inv",
    )(gram)


HBM = pl.BlockSpec(memory_space=pltpu.HBM)
VMEM = pl.BlockSpec(memory_space=pltpu.VMEM)
SMEM = pl.BlockSpec(memory_space=pltpu.SMEM)


def scalar(value):
    return value.astype(jnp.int32).reshape(1)


def sketch_kernel(core_ref, m_ref, o_ref, p_ref, send_ref, sem):
    half = send_ref.shape[1]
    at = pl.multiple_of((1 - core_ref[0]) * half, half)
    copy = pltpu.make_async_copy(m_ref.at[:, pl.ds(at, half)], send_ref, sem)
    copy.start()
    p_ref[...] = jnp.dot(m_ref[...], o_ref[...], preferred_element_type=F32)
    copy.wait()


def sketch(matrix, omega, core):
    rows, cols = matrix.shape
    return pl.pallas_call(
        sketch_kernel,
        in_specs=[SMEM, VMEM, VMEM],
        out_specs=[VMEM, VMEM],
        out_shape=[
            jax.ShapeDtypeStruct((rows, K), F32),
            jax.ShapeDtypeStruct((rows, cols // 2), BF16),
        ],
        scratch_shapes=[pltpu.SemaphoreType.DMA],
        compiler_params=room(16),
        name="sketch",
    )(scalar(core), matrix, omega)


def share_kernel(parts_ref, out_ref):
    terms = [parts_ref[k] for k in range(parts_ref.shape[0])]
    while len(terms) > 1:
        terms = [terms[i] + terms[i + 1] for i in range(0, len(terms), 2)]
    for k in range(out_ref.shape[0]):
        out_ref[k] = terms[0]


def share(parts, copies):
    return pl.pallas_call(
        share_kernel,
        in_specs=[VMEM],
        out_specs=VMEM,
        out_shape=jax.ShapeDtypeStruct((copies, *parts.shape[1:]), F32),
        compiler_params=room(4),
        name="share",
    )(parts)


def w_kernel(core_ref, s_ref, m_ref, his_ref, gram_ref, w_ref):
    rows, half = his_ref.shape
    width = w_ref.shape[2]
    both = s_ref[...]
    gram_ref[...] = lax.dot_general(
        both, both, (((0,), (0,)), ((), ())), precision=HIGH, preferred_element_type=F32
    )
    core = core_ref[0]
    terms = []
    for who in (core, 1 - core):
        turned = s_ref[pl.ds(pl.multiple_of(who * rows, rows), rows), :].T
        high = turned.astype(BF16)
        low = (turned - high.astype(F32)).astype(BF16)
        terms.append(jnp.concatenate([high, low], axis=0))
    for y in range(NY):
        at = pl.multiple_of(core * half + y * width, width)
        w = jnp.dot(terms[0], m_ref[:, pl.ds(at, width)], preferred_element_type=F32)
        cut = slice(y * width, (y + 1) * width)
        w = w + jnp.dot(terms[1], his_ref[:, cut], preferred_element_type=F32)
        w_ref[y] = w[:K] + w[K:]


def sketch_rows(both, matrix, his, core):
    width = his.shape[1] // NY
    return pl.pallas_call(
        w_kernel,
        in_specs=[SMEM, VMEM, VMEM, VMEM],
        out_specs=[VMEM, VMEM],
        out_shape=[
            jax.ShapeDtypeStruct((K, K), F32),
            jax.ShapeDtypeStruct((NY, K, width), F32),
        ],
        compiler_params=room(20),
        name="sketch_rows",
    )(scalar(core), both, matrix, his)


def finish_kernel(inv_ref, parts_ref, out_ref, held, sems):
    copies = [pltpu.make_async_copy(parts_ref.at[k], held.at[k], sems.at[k]) for k in range(NY)]
    for copy in copies:
        copy.start()
    copies[0].wait()
    total = held[0]
    for k in range(1, NY):
        copies[k].wait()
        total = total + held[k]
    piece = jnp.dot(inv_ref[...], total, precision=HIGH, preferred_element_type=F32).astype(BF16)
    for k in range(NY):
        out_ref[k] = piece


def finish(inverse, parts):
    return pl.pallas_call(
        finish_kernel,
        in_specs=[VMEM, pl.BlockSpec(memory_space=pl.ANY)],
        out_specs=VMEM,
        out_shape=jax.ShapeDtypeStruct(parts.shape, BF16),
        scratch_shapes=[pltpu.VMEM(parts.shape, F32), pltpu.SemaphoreType.DMA((NY,))],
        compiler_params=room(8),
        name="finish",
    )(inverse, parts)


def place_kernel(core_ref, own_ref, other_ref, out_ref, sems):
    width = own_ref.shape[2]
    core = core_ref[0]
    copies = []
    for i, (half, ref) in enumerate(((core, own_ref), (1 - core, other_ref))):
        for y in range(NY):
            at = pl.multiple_of((half * NY + y) * width, width)
            copies.append(
                pltpu.make_async_copy(ref.at[y], out_ref.at[:, pl.ds(at, width)], sems.at[i, y])
            )
    for copy in copies:
        copy.start()
    for copy in copies:
        copy.wait()


def place(own, other, core):
    anywhere = pl.BlockSpec(memory_space=pl.ANY)
    return pl.pallas_call(
        place_kernel,
        in_specs=[SMEM, anywhere, anywhere],
        out_specs=HBM,
        out_shape=jax.ShapeDtypeStruct((K, NROW * own.shape[2]), BF16),
        scratch_shapes=[pltpu.SemaphoreType.DMA((2, NY))],
        compiler_params=room(4),
        name="place",
    )(scalar(core), own, other)


SWAP = [(i, i ^ 1) for i in range(NROW)]
Y_GROUPS = [[2 * k + core for k in range(NY)] for core in range(2)]
CHIP_GROUPS = [
    [(2 * y + core) * NCOL + c for core in range(2) for c in range(NCOL)] for y in range(NY)
]


def local(matrix, omega):
    core = lax.axis_index("row") % 2
    rows = matrix.shape[0]

    partial_value, send = sketch(matrix, omega, core)
    parts = lax.all_to_all(partial_value.reshape(NCOL, rows // NCOL, K), "col", 0, 0)
    his = lax.ppermute(send, "row", SWAP)
    both = lax.all_to_all(
        share(parts, 2 * NCOL), ("row", "col"), 0, 0, axis_index_groups=CHIP_GROUPS
    ).reshape(2 * rows, K)

    gram, w = sketch_rows(both, matrix, his, core)
    parts = lax.all_to_all(w, "row", 0, 0, axis_index_groups=Y_GROUPS)
    for step in (1, 2, 4):
        gram = gram + lax.ppermute(gram, "row", [(i, i ^ (2 * step)) for i in range(NROW)])
    inverse = chol_inv(gram)

    pieces = lax.all_to_all(finish(inverse, parts), "row", 0, 0, axis_index_groups=Y_GROUPS)
    sampled = lax.dynamic_slice_in_dim(both, core * rows, rows, 0)
    basis = lax.dot_general(sampled, inverse, (((1,), (1,)), ((), ())), precision=HIGH).astype(BF16)
    return basis, place(pieces, lax.ppermute(pieces, "row", SWAP), core)


def solution(mesh):
    return jax.shard_map(
        local,
        mesh=mesh,
        in_specs=(P("row", "col"), P("col", None)),
        out_specs=(P("row", None), P(None, "col")),
        check_vma=False,
    )
```

```python
import jax
import jax.numpy as jnp
from jax import lax
from jax.experimental import pallas as pl
from jax.experimental.pallas import tpu as pltpu
from jax.sharding import PartitionSpec as P

K = 128
T = 8
NP = K // T
NX, NY, NZ = 4, 8, 8
NROW, NCOL = 16, 32
F32 = jnp.float32
BF16 = jnp.bfloat16
HIGH = lax.Precision.HIGHEST


def room(mib):
    return pltpu.CompilerParams(vmem_limit_bytes=mib << 20)


def sub_row(x, i):
    return jnp.broadcast_to(x[i : i + 1, :], (T, K))


def lane_col(x, i):
    return jnp.broadcast_to(x[:, i : i + 1], (T, K))


def chol_inv_kernel(z_ref, g_ref, o_ref):
    z = z_ref[0]
    sub = lax.broadcasted_iota(jnp.int32, (T, K), 0)
    lane = lax.broadcasted_iota(jnp.int32, (T, K), 1)
    per = g_ref.shape[1] // T
    a = [g_ref[(p // per) ^ z, (p % per) * T : (p % per + 1) * T, :] for p in range(NP)]
    for k in range(NP):
        lo = k * T
        inside = (lane >= lo) & (lane < lo + T)
        c = [lane_col(a[k], lo + j) for j in range(T)]
        x = jnp.where(inside, jnp.where(lane - lo == sub, 1.0, 0.0), a[k])
        u = x
        dvec = c[0]
        for j in range(T):
            at = sub == j
            d = sub_row(c[j], j)
            r = 1.0 / d
            u = jnp.where(at, x, u)
            dvec = jnp.where(at, d, dvec)
            xj = sub_row(x, j)
            cj = c[j]
            x = jnp.where(at, xj * r, x - (cj * xj) * r)
            for l in range(j + 1, T):
                cl = sub_row(c[l], j)
                c[l] = jnp.where(at, cl * r, c[l] - (cj * cl) * r)
        rows = [sub_row(x, j) for j in range(T)]
        for p in range(k + 1, NP):
            terms = [lane_col(a[p], lo + j) * rows[j] for j in range(T)]
            while len(terms) > 1:
                terms = [terms[i] + terms[i + 1] for i in range(0, len(terms), 2)]
            a[p] = jnp.where(inside, 0.0, a[p]) - terms[0]
        o_ref[lo : lo + T, :] = jnp.where(lane <= lo + sub, u * lax.rsqrt(dvec), 0.0)


HBM = pl.BlockSpec(memory_space=pltpu.HBM)
VMEM = pl.BlockSpec(memory_space=pltpu.VMEM)
SMEM = pl.BlockSpec(memory_space=pltpu.SMEM)
STEPS = 8


def scalar(value):
    return value.astype(jnp.int32).reshape(1)


def chol_inv(strips, z):
    return pl.pallas_call(
        chol_inv_kernel,
        in_specs=[SMEM, VMEM],
        out_specs=VMEM,
        out_shape=jax.ShapeDtypeStruct((K, K), F32),
        compiler_params=room(4),
        name="chol_inv",
    )(scalar(z), strips)


def sketch_kernel(m_ref, o_ref, p_ref, held, omega, m_sems, o_sems):
    depth = omega.shape[1]
    copies = []
    for k in range(STEPS):
        cut = pl.ds(k * depth, depth)
        copies.append(pltpu.make_async_copy(o_ref.at[cut, :], omega.at[k], o_sems.at[k]))
        copies.append(pltpu.make_async_copy(m_ref.at[:, cut], held.at[k], m_sems.at[k]))
    for copy in copies:
        copy.start()
    for k in range(STEPS):
        copies[2 * k].wait()
        copies[2 * k + 1].wait()
        term = jnp.dot(held[k], omega[k], preferred_element_type=F32)
        if k == 0:
            p_ref[...] = term
        else:
            p_ref[...] += term


def sketch(matrix, omega):
    rows, cols = matrix.shape
    depth = cols // STEPS
    return pl.pallas_call(
        sketch_kernel,
        in_specs=[HBM, HBM],
        out_specs=VMEM,
        out_shape=jax.ShapeDtypeStruct((rows, K), F32),
        scratch_shapes=[
            pltpu.VMEM((STEPS, rows, depth), BF16),
            pltpu.VMEM((STEPS, depth, K), BF16),
            pltpu.SemaphoreType.DMA((STEPS,)),
            pltpu.SemaphoreType.DMA((STEPS,)),
        ],
        compiler_params=room(56),
        name="sketch",
    )(matrix, omega)


def share_kernel(parts_ref, out_ref):
    terms = [parts_ref[k] for k in range(parts_ref.shape[0])]
    while len(terms) > 1:
        terms = [terms[i] + terms[i + 1] for i in range(0, len(terms), 2)]
    for k in range(out_ref.shape[0]):
        out_ref[k] = terms[0]


def share(parts, copies):
    return pl.pallas_call(
        share_kernel,
        in_specs=[VMEM],
        out_specs=VMEM,
        out_shape=jax.ShapeDtypeStruct((copies, *parts.shape[1:]), F32),
        compiler_params=room(4),
        cost_estimate=pl.CostEstimate(flops=2_500_000_000, bytes_accessed=8 << 20, transcendentals=0),
        name="share",
    )(parts)


def gram_kernel(z_ref, s_ref, out_ref, held):
    held[...] = lax.dot_general(
        s_ref[...], s_ref[...], (((0,), (0,)), ((), ())), precision=HIGH, preferred_element_type=F32
    )
    tall = out_ref.shape[1]
    strip = held[pl.ds(pl.multiple_of(z_ref[0] * tall, tall), tall), :]
    for k in range(NROW):
        out_ref[k] = strip


def gram_strips(sampled, z):
    return pl.pallas_call(
        gram_kernel,
        in_specs=[SMEM, VMEM],
        out_specs=VMEM,
        out_shape=jax.ShapeDtypeStruct((NROW, K // NZ, K), F32),
        scratch_shapes=[pltpu.VMEM((K, K), F32)],
        compiler_params=room(8),
        cost_estimate=pl.CostEstimate(flops=2_500_000_000, bytes_accessed=8 << 20, transcendentals=0),
        name="gram_strips",
    )(scalar(z), sampled)


def w_kernel(core_ref, s_ref, m_ref, own_ref, other_ref):
    turned = s_ref[...].T
    high = turned.astype(BF16)
    low = (turned - high.astype(F32)).astype(BF16)
    hl = jnp.concatenate([high, low], axis=0)
    width = own_ref.shape[2]
    core = core_ref[0]
    for half, out_ref in ((1 - core, other_ref), (core, own_ref)):
        for y in range(NY):
            at = pl.multiple_of((half * NY + y) * width, width)
            w = jnp.dot(hl, m_ref[:, pl.ds(at, width)], preferred_element_type=F32)
            out_ref[y] = w[:K] + w[K:]


def sketch_rows(sampled, matrix, core):
    width = matrix.shape[1] // NROW
    return pl.pallas_call(
        w_kernel,
        in_specs=[SMEM, VMEM, VMEM],
        out_specs=[VMEM, VMEM],
        out_shape=[jax.ShapeDtypeStruct((NY, K, width), F32)] * 2,
        compiler_params=room(20),
        name="sketch_rows",
    )(scalar(core), sampled, matrix)


def finish_kernel(inv_ref, parts_ref, out_ref, held, sems):
    copies = [pltpu.make_async_copy(parts_ref.at[k], held.at[k], sems.at[k]) for k in range(NY)]
    for copy in copies:
        copy.start()
    copies[0].wait()
    total = held[0]
    for k in range(1, NY):
        copies[k].wait()
        total = total + held[k]
    piece = jnp.dot(inv_ref[...], total, precision=HIGH, preferred_element_type=F32).astype(BF16)
    for k in range(NY):
        out_ref[k] = piece


def finish(inverse, parts):
    return pl.pallas_call(
        finish_kernel,
        in_specs=[VMEM, pl.BlockSpec(memory_space=pl.ANY)],
        out_specs=VMEM,
        out_shape=jax.ShapeDtypeStruct(parts.shape, BF16),
        scratch_shapes=[pltpu.VMEM(parts.shape, F32), pltpu.SemaphoreType.DMA((NY,))],
        compiler_params=room(8),
        name="finish",
    )(inverse, parts)


def place_kernel(core_ref, own_ref, other_ref, out_ref, sems):
    width = own_ref.shape[2]
    core = core_ref[0]
    copies = []
    for i, (half, ref) in enumerate(((core, own_ref), (1 - core, other_ref))):
        for y in range(NY):
            at = pl.multiple_of((half * NY + y) * width, width)
            copies.append(
                pltpu.make_async_copy(ref.at[y], out_ref.at[:, pl.ds(at, width)], sems.at[i, y])
            )
    for copy in copies:
        copy.start()
    for copy in copies:
        copy.wait()


def place(own, other, core):
    anywhere = pl.BlockSpec(memory_space=pl.ANY)
    return pl.pallas_call(
        place_kernel,
        in_specs=[SMEM, anywhere, anywhere],
        out_specs=HBM,
        out_shape=jax.ShapeDtypeStruct((K, NROW * own.shape[2]), BF16),
        scratch_shapes=[pltpu.SemaphoreType.DMA((2, NY))],
        compiler_params=room(4),
        name="place",
    )(scalar(core), own, other)


SWAP = [(i, i ^ 1) for i in range(NROW)]
Y_GROUPS = [[2 * k + core for k in range(NY)] for core in range(2)]


def local(matrix, omega):
    core = lax.axis_index("row") % 2
    z = lax.axis_index("col") % NZ
    rows = matrix.shape[0]

    partial_value = sketch(matrix, omega)
    parts = lax.all_to_all(partial_value.reshape(NCOL, rows // NCOL, K), "col", 0, 0)
    sampled = lax.all_to_all(share(parts, NCOL), "col", 0, 0).reshape(rows, K)

    strips = gram_strips(sampled, z)
    held, strips = lax.optimization_barrier((sampled, strips))
    strips = share(lax.all_to_all(strips, "row", 0, 0), 1)
    own, other = sketch_rows(held, matrix, core)
    mine = own + lax.ppermute(other, "row", SWAP)
    parts = lax.all_to_all(mine, "row", 0, 0, axis_index_groups=Y_GROUPS)
    for step in (1, 2, 4):
        theirs = lax.ppermute(strips, "col", [(i, i ^ step) for i in range(NCOL)])
        strips = jnp.concatenate([strips, theirs], axis=0)
    inverse = chol_inv(strips, z)

    pieces = lax.all_to_all(finish(inverse, parts), "row", 0, 0, axis_index_groups=Y_GROUPS)
    basis = lax.dot_general(sampled, inverse, (((1,), (1,)), ((), ())), precision=HIGH).astype(BF16)
    return basis, place(pieces, lax.ppermute(pieces, "row", SWAP), core)


def solution(mesh):
    return jax.shard_map(
        local,
        mesh=mesh,
        in_specs=(P("row", "col"), P("col", None)),
        out_specs=(P("row", None), P(None, "col")),
        check_vma=False,
    )
```

```python
import jax
import jax.numpy as jnp
from jax import lax
from jax.experimental import pallas as pl
from jax.experimental.pallas import tpu as pltpu
from jax.sharding import PartitionSpec as P

K = 128
T = 8
NP = K // T
NX, NY, NZ = 4, 8, 8
NROW, NCOL = 16, 32
F32 = jnp.float32
BF16 = jnp.bfloat16
HIGH = lax.Precision.HIGHEST


def room(mib):
    return pltpu.CompilerParams(vmem_limit_bytes=mib << 20)


def sub_row(x, i):
    return jnp.broadcast_to(x[i : i + 1, :], (T, K))


def lane_col(x, i):
    return jnp.broadcast_to(x[:, i : i + 1], (T, K))


def chol_inv_kernel(z_ref, g_ref, o_ref, q_ref):
    z = z_ref[0]
    sub = lax.broadcasted_iota(jnp.int32, (T, K), 0)
    lane = lax.broadcasted_iota(jnp.int32, (T, K), 1)
    per = g_ref.shape[1] // T
    a = [g_ref[(p // per) ^ z, (p % per) * T : (p % per + 1) * T, :] for p in range(NP)]
    squares = jnp.zeros((T, K), F32)
    diagonal = jnp.zeros((T, K), F32)
    for p in range(NP):
        diagonal = jnp.where(lane == p * T + sub, a[p], diagonal)
    for k in range(NP):
        lo = k * T
        inside = (lane >= lo) & (lane < lo + T)
        c = [lane_col(a[k], lo + j) for j in range(T)]
        x = jnp.where(inside, jnp.where(lane - lo == sub, 1.0, 0.0), a[k])
        u = x
        dvec = c[0]
        for j in range(T):
            at = sub == j
            d = sub_row(c[j], j)
            r = 1.0 / d
            u = jnp.where(at, x, u)
            dvec = jnp.where(at, d, dvec)
            xj = sub_row(x, j)
            cj = c[j]
            x = jnp.where(at, xj * r, x - (cj * xj) * r)
            for l in range(j + 1, T):
                cl = sub_row(c[l], j)
                c[l] = jnp.where(at, cl * r, c[l] - (cj * cl) * r)
        rows = [sub_row(x, j) for j in range(T)]
        for p in range(k + 1, NP):
            terms = [lane_col(a[p], lo + j) * rows[j] for j in range(T)]
            while len(terms) > 1:
                terms = [terms[i] + terms[i + 1] for i in range(0, len(terms), 2)]
            a[p] = jnp.where(inside, 0.0, a[p]) - terms[0]
        done = jnp.where(lane <= lo + sub, u * lax.rsqrt(dvec), 0.0)
        o_ref[lo : lo + T, :] = done
        squares = squares + done * done
    q_ref[...] = squares * jnp.sum(diagonal, axis=0, keepdims=True)


HBM = pl.BlockSpec(memory_space=pltpu.HBM)
VMEM = pl.BlockSpec(memory_space=pltpu.VMEM)
SMEM = pl.BlockSpec(memory_space=pltpu.SMEM)
STEPS = 4
STRIPS = 4


def scalar(value):
    return value.astype(jnp.int32).reshape(1)


def chol_inv(strips, z):
    return pl.pallas_call(
        chol_inv_kernel,
        in_specs=[SMEM, VMEM],
        out_specs=[VMEM, VMEM],
        out_shape=[jax.ShapeDtypeStruct((K, K), F32), jax.ShapeDtypeStruct((T, K), F32)],
        compiler_params=room(4),
        name="chol_inv",
    )(scalar(z), strips)


def sketch_kernel(m_ref, o_ref, p_ref, held, omega, m_sems, o_sems):
    depth = omega.shape[1]
    copies = []
    for k in range(STEPS):
        cut = pl.ds(k * depth, depth)
        copies.append(pltpu.make_async_copy(o_ref.at[cut, :], omega.at[k], o_sems.at[k]))
        copies.append(pltpu.make_async_copy(m_ref.at[:, cut], held.at[k], m_sems.at[k]))
    for copy in copies:
        copy.start()
    for k in range(STEPS):
        copies[2 * k].wait()
        copies[2 * k + 1].wait()
        term = jnp.dot(held[k], omega[k], preferred_element_type=F32)
        if k == 0:
            p_ref[...] = term
        else:
            p_ref[...] += term


def sketch(matrix, omega):
    rows, cols = matrix.shape
    depth = cols // STEPS
    return pl.pallas_call(
        sketch_kernel,
        in_specs=[HBM, HBM],
        out_specs=VMEM,
        out_shape=jax.ShapeDtypeStruct((rows, K), F32),
        scratch_shapes=[
            pltpu.VMEM((STEPS, rows, depth), BF16),
            pltpu.VMEM((STEPS, depth, K), BF16),
            pltpu.SemaphoreType.DMA((STEPS,)),
            pltpu.SemaphoreType.DMA((STEPS,)),
        ],
        compiler_params=room(56),
        name="sketch",
    )(matrix, omega)


def share_kernel(parts_ref, out_ref):
    terms = [parts_ref[k] for k in range(parts_ref.shape[0])]
    while len(terms) > 1:
        terms = [terms[i] + terms[i + 1] for i in range(0, len(terms), 2)]
    for k in range(out_ref.shape[0]):
        out_ref[k] = terms[0]


def share(parts, copies):
    return pl.pallas_call(
        share_kernel,
        in_specs=[VMEM],
        out_specs=VMEM,
        out_shape=jax.ShapeDtypeStruct((copies, *parts.shape[1:]), F32),
        compiler_params=room(4),
        cost_estimate=pl.CostEstimate(flops=2_500_000_000, bytes_accessed=8 << 20, transcendentals=0),
        name="share",
    )(parts)


def gram_kernel(z_ref, s_ref, out_ref, held):
    held[...] = lax.dot_general(
        s_ref[...], s_ref[...], (((0,), (0,)), ((), ())), precision=HIGH, preferred_element_type=F32
    )
    tall = out_ref.shape[1]
    strip = held[pl.ds(pl.multiple_of(z_ref[0] * tall, tall), tall), :]
    for k in range(NROW):
        out_ref[k] = strip


def gram_strips(sampled, z):
    return pl.pallas_call(
        gram_kernel,
        in_specs=[SMEM, VMEM],
        out_specs=VMEM,
        out_shape=jax.ShapeDtypeStruct((NROW, K // STRIPS, K), F32),
        scratch_shapes=[pltpu.VMEM((K, K), F32)],
        compiler_params=room(8),
        cost_estimate=pl.CostEstimate(flops=2_500_000_000, bytes_accessed=8 << 20, transcendentals=0),
        name="gram_strips",
    )(scalar(z), sampled)


def w_kernel(core_ref, s_ref, m_ref, own_ref, other_ref):
    turned = s_ref[...].T
    high = turned.astype(BF16)
    low = (turned - high.astype(F32)).astype(BF16)
    hl = jnp.concatenate([high, low], axis=0)
    width = own_ref.shape[2]
    core = core_ref[0]
    for half, out_ref in ((1 - core, other_ref), (core, own_ref)):
        for y in range(NY):
            at = pl.multiple_of((half * NY + y) * width, width)
            w = jnp.dot(hl, m_ref[:, pl.ds(at, width)], preferred_element_type=F32)
            out_ref[y] = w[:K] + w[K:]


def sketch_rows(sampled, matrix, core):
    width = matrix.shape[1] // NROW
    return pl.pallas_call(
        w_kernel,
        in_specs=[SMEM, VMEM, VMEM],
        out_specs=[VMEM, VMEM],
        out_shape=[jax.ShapeDtypeStruct((NY, K, width), F32)] * 2,
        compiler_params=room(20),
        name="sketch_rows",
    )(scalar(core), sampled, matrix)


def fold_kernel(a_ref, b_ref, high_ref, low_ref):
    for y in range(NY):
        w = a_ref[y] + b_ref[y]
        high = w.astype(BF16)
        high_ref[y] = high
        low_ref[y] = (w - high.astype(F32)).astype(BF16)


def fold(a, b):
    return pl.pallas_call(
        fold_kernel,
        in_specs=[VMEM, VMEM],
        out_specs=[VMEM, VMEM],
        out_shape=[jax.ShapeDtypeStruct(a.shape, BF16)] * 2,
        compiler_params=room(8),
        name="fold",
    )(a, b)


def finish_kernel(inv_ref, *refs):
    out_ref = refs[-1]
    terms = [ref[k].astype(F32) for ref in refs[:-1] for k in range(NY)]
    while len(terms) > 1:
        terms = [terms[i] + terms[i + 1] for i in range(0, len(terms), 2)]
    piece = jnp.dot(inv_ref[...], terms[0], precision=HIGH, preferred_element_type=F32).astype(BF16)
    for k in range(NY):
        out_ref[k] = piece


def finish(inverse, *parts):
    return pl.pallas_call(
        finish_kernel,
        in_specs=[VMEM] * (1 + len(parts)),
        out_specs=VMEM,
        out_shape=jax.ShapeDtypeStruct(parts[0].shape, BF16),
        compiler_params=room(8),
        name="finish",
    )(inverse, *parts)


def place_kernel(core_ref, own_ref, other_ref, out_ref, sems):
    width = own_ref.shape[2]
    core = core_ref[0]
    copies = []
    for i, (half, ref) in enumerate(((core, own_ref), (1 - core, other_ref))):
        for y in range(NY):
            at = pl.multiple_of((half * NY + y) * width, width)
            copies.append(
                pltpu.make_async_copy(ref.at[y], out_ref.at[:, pl.ds(at, width)], sems.at[i, y])
            )
    for copy in copies:
        copy.start()
    for copy in copies:
        copy.wait()


def place(own, other, core):
    anywhere = pl.BlockSpec(memory_space=pl.ANY)
    return pl.pallas_call(
        place_kernel,
        in_specs=[SMEM, anywhere, anywhere],
        out_specs=HBM,
        out_shape=jax.ShapeDtypeStruct((K, NROW * own.shape[2]), BF16),
        scratch_shapes=[pltpu.SemaphoreType.DMA((2, NY))],
        compiler_params=room(4),
        name="place",
    )(scalar(core), own, other)


SWAP = [(i, i ^ 1) for i in range(NROW)]
Y_GROUPS = [[2 * k + core for k in range(NY)] for core in range(2)]


def over_y(blocks):
    return lax.all_to_all(blocks, "row", 0, 0, axis_index_groups=Y_GROUPS)


def local(matrix, omega):
    core = lax.axis_index("row") % 2
    z = lax.axis_index("col") % NZ // 2
    rows = matrix.shape[0]

    partial_value = sketch(matrix, omega)
    parts = lax.all_to_all(partial_value.reshape(NCOL, rows // NCOL, K), "col", 0, 0)
    sampled = lax.all_to_all(share(parts, NCOL), "col", 0, 0).reshape(rows, K)

    strips = gram_strips(sampled, z)
    held, strips = lax.optimization_barrier((sampled, strips))
    strips = share(lax.all_to_all(strips, "row", 0, 0), 1)
    own, other = sketch_rows(held, matrix, core)
    high, low = fold(own, lax.ppermute(other, "row", SWAP))
    parts = over_y(high)
    for step in (2, 4):
        theirs = lax.ppermute(strips, "col", [(i, i ^ step) for i in range(NCOL)])
        strips = jnp.concatenate([strips, theirs], axis=0)
    inverse, growth = chol_inv(strips, z)

    pieces = lax.cond(
        jnp.sum(growth) <= 2.0 * K,
        lambda: finish(inverse, parts),
        lambda: finish(inverse, parts, over_y(low)),
    )
    pieces = over_y(pieces)
    basis = lax.dot_general(sampled, inverse, (((1,), (1,)), ((), ())), precision=HIGH).astype(BF16)
    return basis, place(pieces, lax.ppermute(pieces, "row", SWAP), core)


def solution(mesh):
    return jax.shard_map(
        local,
        mesh=mesh,
        in_specs=(P("row", "col"), P("col", None)),
        out_specs=(P("row", None), P(None, "col")),
        check_vma=False,
    )
```

```python
import jax
import jax.numpy as jnp
from jax import lax
from jax.experimental import pallas as pl
from jax.experimental.pallas import tpu as pltpu
from jax.sharding import PartitionSpec as P

K = 128
T = 8
NP = K // T
NX, NY, NZ = 4, 8, 8
NROW, NCOL = 16, 32
F32 = jnp.float32
BF16 = jnp.bfloat16
HIGH = lax.Precision.HIGHEST


def room(mib):
    return pltpu.CompilerParams(vmem_limit_bytes=mib << 20)


def sub_row(x, i):
    return jnp.broadcast_to(x[i : i + 1, :], (T, K))


def lane_col(x, i):
    return jnp.broadcast_to(x[:, i : i + 1], (T, K))


def chol_inv_kernel(z_ref, g_ref, o_ref, q_ref):
    z = z_ref[0]
    sub = lax.broadcasted_iota(jnp.int32, (T, K), 0)
    lane = lax.broadcasted_iota(jnp.int32, (T, K), 1)
    per = g_ref.shape[1] // T
    a = [g_ref[(p // per) ^ z, (p % per) * T : (p % per + 1) * T, :] for p in range(NP)]
    squares = jnp.zeros((T, K), F32)
    diagonal = jnp.zeros((T, K), F32)
    for p in range(NP):
        diagonal = jnp.where(lane == p * T + sub, a[p], diagonal)
    for k in range(NP):
        lo = k * T
        inside = (lane >= lo) & (lane < lo + T)
        c = [lane_col(a[k], lo + j) for j in range(T)]
        x = jnp.where(inside, jnp.where(lane - lo == sub, 1.0, 0.0), a[k])
        u = x
        dvec = c[0]
        for j in range(T):
            at = sub == j
            d = sub_row(c[j], j)
            r = 1.0 / d
            u = jnp.where(at, x, u)
            dvec = jnp.where(at, d, dvec)
            xj = sub_row(x, j)
            cj = c[j]
            x = jnp.where(at, xj * r, x - (cj * xj) * r)
            for l in range(j + 1, T):
                cl = sub_row(c[l], j)
                c[l] = jnp.where(at, cl * r, c[l] - (cj * cl) * r)
        rows = [sub_row(x, j) for j in range(T)]
        for p in range(k + 1, NP):
            terms = [lane_col(a[p], lo + j) * rows[j] for j in range(T)]
            while len(terms) > 1:
                terms = [terms[i] + terms[i + 1] for i in range(0, len(terms), 2)]
            a[p] = jnp.where(inside, 0.0, a[p]) - terms[0]
        done = jnp.where(lane <= lo + sub, u * lax.rsqrt(dvec), 0.0)
        o_ref[lo : lo + T, :] = done
        squares = squares + done * done
    q_ref[0, 0] = jnp.sum(squares * jnp.sum(diagonal, axis=0, keepdims=True))


HBM = pl.BlockSpec(memory_space=pltpu.HBM)
VMEM = pl.BlockSpec(memory_space=pltpu.VMEM)
SMEM = pl.BlockSpec(memory_space=pltpu.SMEM)
STEPS = 4
STRIPS = 4
SWAPS = 2


def scalar(value):
    return value.astype(jnp.int32).reshape(1)


def chol_inv(strips, z):
    return pl.pallas_call(
        chol_inv_kernel,
        in_specs=[SMEM, VMEM],
        out_specs=[VMEM, SMEM],
        out_shape=[jax.ShapeDtypeStruct((K, K), F32), jax.ShapeDtypeStruct((1, 1), F32)],
        compiler_params=room(4),
        name="chol_inv",
    )(scalar(z), strips)


def sketch_kernel(m_ref, o_ref, p_ref, held, omega, m_sems, o_sems):
    depth = omega.shape[1]
    copies = []
    for k in range(STEPS):
        cut = pl.ds(k * depth, depth)
        copies.append(pltpu.make_async_copy(o_ref.at[cut, :], omega.at[k], o_sems.at[k]))
        copies.append(pltpu.make_async_copy(m_ref.at[:, cut], held.at[k], m_sems.at[k]))
    for copy in copies:
        copy.start()
    for k in range(STEPS):
        copies[2 * k].wait()
        copies[2 * k + 1].wait()
        term = jnp.dot(held[k], omega[k], preferred_element_type=F32)
        if k == 0:
            p_ref[...] = term
        else:
            p_ref[...] += term


def sketch(matrix, omega):
    rows, cols = matrix.shape
    depth = cols // STEPS
    return pl.pallas_call(
        sketch_kernel,
        in_specs=[HBM, HBM],
        out_specs=VMEM,
        out_shape=jax.ShapeDtypeStruct((rows, K), F32),
        scratch_shapes=[
            pltpu.VMEM((STEPS, rows, depth), BF16),
            pltpu.VMEM((STEPS, depth, K), BF16),
            pltpu.SemaphoreType.DMA((STEPS,)),
            pltpu.SemaphoreType.DMA((STEPS,)),
        ],
        compiler_params=room(56),
        name="sketch",
    )(matrix, omega)


def share_kernel(parts_ref, out_ref):
    terms = [parts_ref[k] for k in range(parts_ref.shape[0])]
    while len(terms) > 1:
        terms = [terms[i] + terms[i + 1] for i in range(0, len(terms), 2)]
    for k in range(out_ref.shape[0]):
        out_ref[k] = terms[0]


def share(parts, copies):
    return pl.pallas_call(
        share_kernel,
        in_specs=[VMEM],
        out_specs=VMEM,
        out_shape=jax.ShapeDtypeStruct((copies, *parts.shape[1:]), F32),
        compiler_params=room(4),
        cost_estimate=pl.CostEstimate(flops=2_500_000_000, bytes_accessed=8 << 20, transcendentals=0),
        name="share",
    )(parts)


def gram_kernel(z_ref, s_ref, out_ref, held):
    held[...] = lax.dot_general(
        s_ref[...], s_ref[...], (((0,), (0,)), ((), ())), precision=HIGH, preferred_element_type=F32
    )
    tall = out_ref.shape[1]
    strip = held[pl.ds(pl.multiple_of(z_ref[0] * tall, tall), tall), :]
    for k in range(NROW):
        out_ref[k] = strip


def gram_strips(sampled, z):
    return pl.pallas_call(
        gram_kernel,
        in_specs=[SMEM, VMEM],
        out_specs=VMEM,
        out_shape=jax.ShapeDtypeStruct((NROW, K // STRIPS, K), F32),
        scratch_shapes=[pltpu.VMEM((K, K), F32)],
        compiler_params=room(8),
        cost_estimate=pl.CostEstimate(flops=2_500_000_000, bytes_accessed=8 << 20, transcendentals=0),
        name="gram_strips",
    )(scalar(z), sampled)


def w_kernel(core_ref, s_ref, m_ref, own_ref, low_ref, *high_refs):
    turned = s_ref[...].T
    high = turned.astype(BF16)
    low = (turned - high.astype(F32)).astype(BF16)
    hl = jnp.concatenate([high, low], axis=0)
    width = own_ref.shape[2]
    per = NY // SWAPS
    core = core_ref[0]
    for half, mine in ((1 - core, False), (core, True)):
        for y in range(NY):
            at = pl.multiple_of((half * NY + y) * width, width)
            w = jnp.dot(hl, m_ref[:, pl.ds(at, width)], preferred_element_type=F32)
            w = w[:K] + w[K:]
            if mine:
                own_ref[y] = w
            else:
                lead = w.astype(BF16)
                high_refs[y // per][y % per] = lead
                low_ref[y] = (w - lead.astype(F32)).astype(BF16)


def sketch_rows(sampled, matrix, core):
    width = matrix.shape[1] // NROW
    own, low, *high = pl.pallas_call(
        w_kernel,
        in_specs=[SMEM, VMEM, VMEM],
        out_specs=[VMEM] * (2 + SWAPS),
        out_shape=[
            jax.ShapeDtypeStruct((NY, K, width), F32),
            jax.ShapeDtypeStruct((NY, K, width), BF16),
        ]
        + [jax.ShapeDtypeStruct((NY // SWAPS, K, width), BF16)] * SWAPS,
        compiler_params=room(20),
        name="sketch_rows",
    )(scalar(core), sampled, matrix)
    return own, low, high


def fold_kernel(a_ref, *refs):
    high_ref, rest_ref = refs[-2:]
    per = NY // SWAPS
    for y in range(NY):
        w = a_ref[y] + refs[y // per][y % per].astype(F32)
        high = w.astype(BF16)
        high_ref[y] = high
        rest_ref[y] = w - high.astype(F32)


def fold(a, parts):
    return pl.pallas_call(
        fold_kernel,
        in_specs=[VMEM] * (1 + SWAPS),
        out_specs=[VMEM, VMEM],
        out_shape=[jax.ShapeDtypeStruct(a.shape, BF16), jax.ShapeDtypeStruct(a.shape, F32)],
        compiler_params=room(8),
        name="fold",
    )(a, *parts)


def finish_kernel(inv_ref, *refs):
    out_ref = refs[-1]
    terms = [ref[k].astype(F32) for ref in refs[:-1] for k in range(NY)]
    while len(terms) > 1:
        terms = [terms[i] + terms[i + 1] for i in range(0, len(terms), 2)]
    piece = jnp.dot(inv_ref[...], terms[0], precision=HIGH, preferred_element_type=F32).astype(BF16)
    for k in range(NY):
        out_ref[k] = piece


def finish(inverse, *parts):
    return pl.pallas_call(
        finish_kernel,
        in_specs=[VMEM] * (1 + len(parts)),
        out_specs=VMEM,
        out_shape=jax.ShapeDtypeStruct(parts[0].shape, BF16),
        compiler_params=room(8),
        name="finish",
    )(inverse, *parts)


def place_kernel(core_ref, own_ref, other_ref, out_ref, sems):
    width = own_ref.shape[2]
    core = core_ref[0]
    copies = []
    for i, (half, ref) in enumerate(((core, own_ref), (1 - core, other_ref))):
        for y in range(NY):
            at = pl.multiple_of((half * NY + y) * width, width)
            copies.append(
                pltpu.make_async_copy(ref.at[y], out_ref.at[:, pl.ds(at, width)], sems.at[i, y])
            )
    for copy in copies:
        copy.start()
    for copy in copies:
        copy.wait()


def place(own, other, core):
    anywhere = pl.BlockSpec(memory_space=pl.ANY)
    return pl.pallas_call(
        place_kernel,
        in_specs=[SMEM, anywhere, anywhere],
        out_specs=HBM,
        out_shape=jax.ShapeDtypeStruct((K, NROW * own.shape[2]), BF16),
        scratch_shapes=[pltpu.SemaphoreType.DMA((2, NY))],
        compiler_params=room(4),
        name="place",
    )(scalar(core), own, other)


SWAP = [(i, i ^ 1) for i in range(NROW)]
Y_GROUPS = [[2 * k + core for k in range(NY)] for core in range(2)]


def over_y(blocks):
    return lax.all_to_all(blocks, "row", 0, 0, axis_index_groups=Y_GROUPS)


def local(matrix, omega):
    core = lax.axis_index("row") % 2
    z = lax.axis_index("col") % NZ // 2
    rows = matrix.shape[0]

    partial_value = sketch(matrix, omega)
    parts = lax.all_to_all(partial_value.reshape(NCOL, rows // NCOL, K), "col", 0, 0)
    sampled = lax.all_to_all(share(parts, NCOL), "col", 0, 0).reshape(rows, K)

    strips = gram_strips(sampled, z)
    held, strips = lax.optimization_barrier((sampled, strips))
    strips = share(lax.all_to_all(strips, "row", 0, 0), 1)
    own, low, other = sketch_rows(held, matrix, core)
    high, rest = fold(own, [lax.ppermute(part, "row", SWAP) for part in other])
    parts = over_y(high)
    for step in (2, 4):
        theirs = lax.ppermute(strips, "col", [(i, i ^ step) for i in range(NCOL)])
        strips = jnp.concatenate([strips, theirs], axis=0)
    inverse, growth = chol_inv(strips, z)

    def with_residuals():
        residual = (rest + lax.ppermute(low, "row", SWAP).astype(F32)).astype(BF16)
        return finish(inverse, parts, over_y(residual))

    pieces = lax.cond(
        growth[0, 0] <= 2.0 * K, lambda: finish(inverse, parts), with_residuals
    )
    pieces = over_y(pieces)
    basis = lax.dot_general(sampled, inverse, (((1,), (1,)), ((), ())), precision=HIGH).astype(BF16)
    return basis, place(pieces, lax.ppermute(pieces, "row", SWAP), core)


def solution(mesh):
    return jax.shard_map(
        local,
        mesh=mesh,
        in_specs=(P("row", "col"), P("col", None)),
        out_specs=(P("row", None), P(None, "col")),
        check_vma=False,
    )
```

```python
import jax
import jax.numpy as jnp
from jax import lax
from jax.experimental import pallas as pl
from jax.experimental.pallas import tpu as pltpu
from jax.sharding import PartitionSpec as P

K = 128
T = 8
NP = K // T
NX, NY, NZ = 4, 8, 8
NROW, NCOL = 16, 32
F32 = jnp.float32
BF16 = jnp.bfloat16
HIGH = lax.Precision.HIGHEST


def room(mib):
    return pltpu.CompilerParams(vmem_limit_bytes=mib << 20)


def sub_row(x, i):
    return jnp.broadcast_to(x[i : i + 1, :], (T, K))


def lane_col(x, i):
    return jnp.broadcast_to(x[:, i : i + 1], (T, K))


def chol_inv_kernel(x_ref, g_ref, o_ref, q_ref):
    mine = x_ref[0]
    sub = lax.broadcasted_iota(jnp.int32, (T, K), 0)
    lane = lax.broadcasted_iota(jnp.int32, (T, K), 1)
    per = g_ref.shape[1] // T
    a = [g_ref[(p // per) ^ mine, (p % per) * T : (p % per + 1) * T, :] for p in range(NP)]
    squares = jnp.zeros((T, K), F32)
    diagonal = jnp.zeros((T, K), F32)
    for p in range(NP):
        diagonal = jnp.where(lane == p * T + sub, a[p], diagonal)
    for k in range(NP):
        lo = k * T
        inside = (lane >= lo) & (lane < lo + T)
        c = [lane_col(a[k], lo + j) for j in range(T)]
        x = jnp.where(inside, jnp.where(lane - lo == sub, 1.0, 0.0), a[k])
        u = x
        dvec = c[0]
        for j in range(T):
            at = sub == j
            d = sub_row(c[j], j)
            r = 1.0 / d
            u = jnp.where(at, x, u)
            dvec = jnp.where(at, d, dvec)
            xj = sub_row(x, j)
            cj = c[j]
            x = jnp.where(at, xj * r, x - (cj * xj) * r)
            for l in range(j + 1, T):
                cl = sub_row(c[l], j)
                c[l] = jnp.where(at, cl * r, c[l] - (cj * cl) * r)
        rows = [sub_row(x, j) for j in range(T)]
        for p in range(k + 1, NP):
            terms = [lane_col(a[p], lo + j) * rows[j] for j in range(T)]
            while len(terms) > 1:
                terms = [terms[i] + terms[i + 1] for i in range(0, len(terms), 2)]
            a[p] = jnp.where(inside, 0.0, a[p]) - terms[0]
        done = jnp.where(lane <= lo + sub, u * lax.rsqrt(dvec), 0.0)
        o_ref[lo : lo + T, :] = done
        squares = squares + done * done
    q_ref[0, 0] = jnp.sum(squares * jnp.sum(diagonal, axis=0, keepdims=True))


HBM = pl.BlockSpec(memory_space=pltpu.HBM)
VMEM = pl.BlockSpec(memory_space=pltpu.VMEM)
SMEM = pl.BlockSpec(memory_space=pltpu.SMEM)
STEPS = 4
STRIPS = 4
SWAPS = 2


def scalar(value):
    return value.astype(jnp.int32).reshape(1)


def chol_inv(strips, x):
    return pl.pallas_call(
        chol_inv_kernel,
        in_specs=[SMEM, VMEM],
        out_specs=[VMEM, SMEM],
        out_shape=[jax.ShapeDtypeStruct((K, K), F32), jax.ShapeDtypeStruct((1, 1), F32)],
        compiler_params=room(4),
        name="chol_inv",
    )(scalar(x), strips)


def sketch_kernel(m_ref, o_ref, p_ref, held, omega, m_sems, o_sems):
    depth = omega.shape[1]
    copies = []
    for k in range(STEPS):
        cut = pl.ds(k * depth, depth)
        copies.append(pltpu.make_async_copy(o_ref.at[cut, :], omega.at[k], o_sems.at[k]))
        copies.append(pltpu.make_async_copy(m_ref.at[:, cut], held.at[k], m_sems.at[k]))
    for copy in copies:
        copy.start()
    for k in range(STEPS):
        copies[2 * k].wait()
        copies[2 * k + 1].wait()
        term = jnp.dot(held[k], omega[k], preferred_element_type=F32)
        if k == 0:
            p_ref[...] = term
        else:
            p_ref[...] += term


def sketch(matrix, omega):
    rows, cols = matrix.shape
    depth = cols // STEPS
    return pl.pallas_call(
        sketch_kernel,
        in_specs=[HBM, HBM],
        out_specs=VMEM,
        out_shape=jax.ShapeDtypeStruct((rows, K), F32),
        scratch_shapes=[
            pltpu.VMEM((STEPS, rows, depth), BF16),
            pltpu.VMEM((STEPS, depth, K), BF16),
            pltpu.SemaphoreType.DMA((STEPS,)),
            pltpu.SemaphoreType.DMA((STEPS,)),
        ],
        compiler_params=room(56),
        name="sketch",
    )(matrix, omega)


def share_kernel(parts_ref, out_ref):
    terms = [parts_ref[k] for k in range(parts_ref.shape[0])]
    while len(terms) > 1:
        terms = [terms[i] + terms[i + 1] for i in range(0, len(terms), 2)]
    for k in range(out_ref.shape[0]):
        out_ref[k] = terms[0]


def share(parts, copies):
    return pl.pallas_call(
        share_kernel,
        in_specs=[VMEM],
        out_specs=VMEM,
        out_shape=jax.ShapeDtypeStruct((copies, *parts.shape[1:]), F32),
        compiler_params=room(4),
        cost_estimate=pl.CostEstimate(flops=2_500_000_000, bytes_accessed=8 << 20, transcendentals=0),
        name="share",
    )(parts)


def gram_kernel(x_ref, s_ref, out_ref, held):
    held[...] = lax.dot_general(
        s_ref[...], s_ref[...], (((0,), (0,)), ((), ())), precision=HIGH, preferred_element_type=F32
    )
    tall = out_ref.shape[1]
    strip = held[pl.ds(pl.multiple_of(x_ref[0] * tall, tall), tall), :]
    for k in range(NROW):
        out_ref[k] = strip


def gram_strips(sampled, x):
    return pl.pallas_call(
        gram_kernel,
        in_specs=[SMEM, VMEM],
        out_specs=VMEM,
        out_shape=jax.ShapeDtypeStruct((NROW, K // STRIPS, K), F32),
        scratch_shapes=[pltpu.VMEM((K, K), F32)],
        compiler_params=room(8),
        cost_estimate=pl.CostEstimate(flops=2_500_000_000, bytes_accessed=8 << 20, transcendentals=0),
        name="gram_strips",
    )(scalar(x), sampled)


def w_kernel(core_ref, s_ref, m_ref, own_ref, low_ref, *high_refs):
    turned = s_ref[...].T
    terms = []
    for _ in range(3):
        terms.append(turned.astype(BF16))
        turned = turned - terms[-1].astype(F32)
    terms = jnp.concatenate(terms, axis=0)
    width = own_ref.shape[2]
    per = NY // SWAPS
    core = core_ref[0]
    for half, mine in ((1 - core, False), (core, True)):
        for y in range(NY):
            at = pl.multiple_of((half * NY + y) * width, width)
            w = jnp.dot(terms, m_ref[:, pl.ds(at, width)], preferred_element_type=F32)
            w = w[:K] + (w[K : 2 * K] + w[2 * K :])
            if mine:
                own_ref[y] = w
            else:
                lead = w.astype(BF16)
                high_refs[y // per][y % per] = lead
                low_ref[y] = w - lead.astype(F32)


def sketch_rows(sampled, matrix, core):
    width = matrix.shape[1] // NROW
    own, low, *high = pl.pallas_call(
        w_kernel,
        in_specs=[SMEM, VMEM, VMEM],
        out_specs=[VMEM] * (2 + SWAPS),
        out_shape=[
            jax.ShapeDtypeStruct((NY, K, width), F32),
            jax.ShapeDtypeStruct((NY, K, width), F32),
        ]
        + [jax.ShapeDtypeStruct((NY // SWAPS, K, width), BF16)] * SWAPS,
        compiler_params=room(20),
        name="sketch_rows",
    )(scalar(core), sampled, matrix)
    return own, low, high


def fold_kernel(a_ref, *refs):
    high_ref, rest_ref = refs[-2:]
    per = NY // SWAPS
    for y in range(NY):
        w = a_ref[y] + refs[y // per][y % per].astype(F32)
        high = w.astype(BF16)
        high_ref[y] = high
        rest_ref[y] = w - high.astype(F32)


def fold(a, parts):
    return pl.pallas_call(
        fold_kernel,
        in_specs=[VMEM] * (1 + SWAPS),
        out_specs=[VMEM, VMEM],
        out_shape=[jax.ShapeDtypeStruct(a.shape, BF16), jax.ShapeDtypeStruct(a.shape, F32)],
        compiler_params=room(8),
        name="fold",
    )(a, *parts)


def finish_kernel(inv_ref, *refs):
    out_ref = refs[-1]
    terms = [ref[k].astype(F32) for ref in refs[:-1] for k in range(NY)]
    while len(terms) > 1:
        terms = [terms[i] + terms[i + 1] for i in range(0, len(terms), 2)]
    piece = jnp.dot(inv_ref[...], terms[0], precision=HIGH, preferred_element_type=F32).astype(BF16)
    for k in range(NY):
        out_ref[k] = piece


def finish(inverse, *parts):
    return pl.pallas_call(
        finish_kernel,
        in_specs=[VMEM] * (1 + len(parts)),
        out_specs=VMEM,
        out_shape=jax.ShapeDtypeStruct(parts[0].shape, BF16),
        compiler_params=room(8),
        name="finish",
    )(inverse, *parts)


def place_kernel(core_ref, own_ref, other_ref, out_ref, sems):
    width = own_ref.shape[2]
    core = core_ref[0]
    copies = []
    for i, (half, ref) in enumerate(((core, own_ref), (1 - core, other_ref))):
        for y in range(NY):
            at = pl.multiple_of((half * NY + y) * width, width)
            copies.append(
                pltpu.make_async_copy(ref.at[y], out_ref.at[:, pl.ds(at, width)], sems.at[i, y])
            )
    for copy in copies:
        copy.start()
    for copy in copies:
        copy.wait()


def place(own, other, core):
    anywhere = pl.BlockSpec(memory_space=pl.ANY)
    return pl.pallas_call(
        place_kernel,
        in_specs=[SMEM, anywhere, anywhere],
        out_specs=HBM,
        out_shape=jax.ShapeDtypeStruct((K, NROW * own.shape[2]), BF16),
        scratch_shapes=[pltpu.SemaphoreType.DMA((2, NY))],
        compiler_params=room(4),
        name="place",
    )(scalar(core), own, other)


SWAP = [(i, i ^ 1) for i in range(NROW)]
Y_GROUPS = [[2 * k + core for k in range(NY)] for core in range(2)]


def over_y(blocks):
    return lax.all_to_all(blocks, "row", 0, 0, axis_index_groups=Y_GROUPS)


def local(matrix, omega):
    core = lax.axis_index("row") % 2
    x = lax.axis_index("col") // NZ
    rows = matrix.shape[0]

    partial_value = sketch(matrix, omega)
    parts = lax.all_to_all(partial_value.reshape(NCOL, rows // NCOL, K), "col", 0, 0)
    sampled = lax.all_to_all(share(parts, NCOL), "col", 0, 0).reshape(rows, K)

    strips = gram_strips(sampled, x)
    held, strips = lax.optimization_barrier((sampled, strips))
    strips = share(lax.all_to_all(strips, "row", 0, 0), 1)
    own, low, other = sketch_rows(held, matrix, core)
    high, rest = fold(own, [lax.ppermute(part, "row", SWAP) for part in other])
    parts = over_y(high)
    for step in (NZ, 2 * NZ):
        theirs = lax.ppermute(strips, "col", [(i, i ^ step) for i in range(NCOL)])
        strips = jnp.concatenate([strips, theirs], axis=0)
    inverse, growth = chol_inv(strips, x)

    def with_residuals():
        return finish(inverse, parts, over_y(rest + lax.ppermute(low, "row", SWAP)))

    pieces = lax.cond(
        growth[0, 0] <= 2.0 * K, lambda: finish(inverse, parts), with_residuals
    )
    pieces = over_y(pieces)
    basis = lax.dot_general(sampled, inverse, (((1,), (1,)), ((), ())), precision=HIGH).astype(BF16)
    return basis, place(pieces, lax.ppermute(pieces, "row", SWAP), core)


def solution(mesh):
    return jax.shard_map(
        local,
        mesh=mesh,
        in_specs=(P("row", "col"), P("col", None)),
        out_specs=(P("row", None), P(None, "col")),
        check_vma=False,
    )
```

```python
import jax
import jax.numpy as jnp
from jax import lax
from jax.experimental import pallas as pl
from jax.experimental.pallas import tpu as pltpu
from jax.sharding import PartitionSpec as P

K = 128
T = 8
NP = K // T
NX, NY, NZ = 4, 8, 8
NROW, NCOL = 16, 32
F32 = jnp.float32
BF16 = jnp.bfloat16
HIGH = lax.Precision.HIGHEST


def room(mib):
    return pltpu.CompilerParams(vmem_limit_bytes=mib << 20)


def sub_row(x, i):
    return jnp.broadcast_to(x[i : i + 1, :], (T, K))


def lane_col(x, i):
    return jnp.broadcast_to(x[:, i : i + 1], (T, K))


def chol_inv_kernel(x_ref, *refs):
    o_ref, q_ref, held = refs[STRIPS:]
    for j in range(STRIPS):
        held[j ^ x_ref[0]] = refs[j][0]
    sub = lax.broadcasted_iota(jnp.int32, (T, K), 0)
    lane = lax.broadcasted_iota(jnp.int32, (T, K), 1)
    per = NP // STRIPS
    a = [held[p // per, (p % per) * T : (p % per + 1) * T, :] for p in range(NP)]
    squares = jnp.zeros((T, K), F32)
    diagonal = jnp.zeros((T, K), F32)
    for p in range(NP):
        diagonal = jnp.where(lane == p * T + sub, a[p], diagonal)
    for k in range(NP):
        lo = k * T
        inside = (lane >= lo) & (lane < lo + T)
        c = [lane_col(a[k], lo + j) for j in range(T)]
        x = jnp.where(inside, jnp.where(lane - lo == sub, 1.0, 0.0), a[k])
        u = x
        dvec = c[0]
        for j in range(T):
            at = sub == j
            d = sub_row(c[j], j)
            r = 1.0 / d
            u = jnp.where(at, x, u)
            dvec = jnp.where(at, d, dvec)
            xj = sub_row(x, j)
            cj = c[j]
            x = jnp.where(at, xj * r, x - (cj * xj) * r)
            for l in range(j + 1, T):
                cl = sub_row(c[l], j)
                c[l] = jnp.where(at, cl * r, c[l] - (cj * cl) * r)
        rows = [sub_row(x, j) for j in range(T)]
        for p in range(k + 1, NP):
            terms = [lane_col(a[p], lo + j) * rows[j] for j in range(T)]
            while len(terms) > 1:
                terms = [terms[i] + terms[i + 1] for i in range(0, len(terms), 2)]
            a[p] = jnp.where(inside, 0.0, a[p]) - terms[0]
        done = jnp.where(lane <= lo + sub, u * lax.rsqrt(dvec), 0.0)
        o_ref[lo : lo + T, :] = done
        squares = squares + done * done
    q_ref[0, 0] = jnp.sum(squares * jnp.sum(diagonal, axis=0, keepdims=True))


HBM = pl.BlockSpec(memory_space=pltpu.HBM)
VMEM = pl.BlockSpec(memory_space=pltpu.VMEM)
SMEM = pl.BlockSpec(memory_space=pltpu.SMEM)
STEPS = 4
STRIPS = 4
SWAPS = 2


def scalar(value):
    return value.astype(jnp.int32).reshape(1)


def chol_inv(strips, x):
    return pl.pallas_call(
        chol_inv_kernel,
        in_specs=[SMEM] + [VMEM] * STRIPS,
        out_specs=[VMEM, SMEM],
        out_shape=[jax.ShapeDtypeStruct((K, K), F32), jax.ShapeDtypeStruct((1, 1), F32)],
        scratch_shapes=[pltpu.VMEM((STRIPS, K // STRIPS, K), F32)],
        compiler_params=room(4),
        name="chol_inv",
    )(scalar(x), *strips)


def sketch_kernel(m_ref, o_ref, p_ref, held, omega, m_sems, o_sems):
    depth = omega.shape[1]
    copies = []
    for k in range(STEPS):
        cut = pl.ds(k * depth, depth)
        copies.append(pltpu.make_async_copy(o_ref.at[cut, :], omega.at[k], o_sems.at[k]))
        copies.append(pltpu.make_async_copy(m_ref.at[:, cut], held.at[k], m_sems.at[k]))
    for copy in copies:
        copy.start()
    for k in range(STEPS):
        copies[2 * k].wait()
        copies[2 * k + 1].wait()
        term = jnp.dot(held[k], omega[k], preferred_element_type=F32)
        if k == 0:
            p_ref[...] = term
        else:
            p_ref[...] += term


def sketch(matrix, omega):
    rows, cols = matrix.shape
    depth = cols // STEPS
    return pl.pallas_call(
        sketch_kernel,
        in_specs=[HBM, HBM],
        out_specs=VMEM,
        out_shape=jax.ShapeDtypeStruct((rows, K), F32),
        scratch_shapes=[
            pltpu.VMEM((STEPS, rows, depth), BF16),
            pltpu.VMEM((STEPS, depth, K), BF16),
            pltpu.SemaphoreType.DMA((STEPS,)),
            pltpu.SemaphoreType.DMA((STEPS,)),
        ],
        compiler_params=room(56),
        name="sketch",
    )(matrix, omega)


def share_kernel(parts_ref, out_ref):
    terms = [parts_ref[k] for k in range(parts_ref.shape[0])]
    while len(terms) > 1:
        terms = [terms[i] + terms[i + 1] for i in range(0, len(terms), 2)]
    for k in range(out_ref.shape[0]):
        out_ref[k] = terms[0]


def share(parts, copies):
    return pl.pallas_call(
        share_kernel,
        in_specs=[VMEM],
        out_specs=VMEM,
        out_shape=jax.ShapeDtypeStruct((copies, *parts.shape[1:]), F32),
        compiler_params=room(4),
        cost_estimate=pl.CostEstimate(flops=2_500_000_000, bytes_accessed=8 << 20, transcendentals=0),
        name="share",
    )(parts)


def gram_kernel(x_ref, s_ref, out_ref, held):
    held[...] = lax.dot_general(
        s_ref[...], s_ref[...], (((0,), (0,)), ((), ())), precision=HIGH, preferred_element_type=F32
    )
    tall = out_ref.shape[1]
    strip = held[pl.ds(pl.multiple_of(x_ref[0] * tall, tall), tall), :]
    for k in range(NROW):
        out_ref[k] = strip


def gram_strips(sampled, x):
    return pl.pallas_call(
        gram_kernel,
        in_specs=[SMEM, VMEM],
        out_specs=VMEM,
        out_shape=jax.ShapeDtypeStruct((NROW, K // STRIPS, K), F32),
        scratch_shapes=[pltpu.VMEM((K, K), F32)],
        compiler_params=room(8),
        cost_estimate=pl.CostEstimate(flops=2_500_000_000, bytes_accessed=8 << 20, transcendentals=0),
        name="gram_strips",
    )(scalar(x), sampled)


def w_kernel(core_ref, s_ref, m_ref, own_ref, low_ref, *high_refs):
    turned = s_ref[...].T
    terms = []
    for _ in range(3):
        terms.append(turned.astype(BF16))
        turned = turned - terms[-1].astype(F32)
    terms = jnp.concatenate(terms, axis=0)
    width = own_ref.shape[2]
    per = NY // SWAPS
    core = core_ref[0]
    for half, mine in ((1 - core, False), (core, True)):
        for y in range(NY):
            at = pl.multiple_of((half * NY + y) * width, width)
            w = jnp.dot(terms, m_ref[:, pl.ds(at, width)], preferred_element_type=F32)
            w = w[:K] + (w[K : 2 * K] + w[2 * K :])
            if mine:
                own_ref[y] = w
            else:
                lead = w.astype(BF16)
                high_refs[y // per][y % per] = lead
                low_ref[y] = w - lead.astype(F32)


def sketch_rows(sampled, matrix, core):
    width = matrix.shape[1] // NROW
    own, low, *high = pl.pallas_call(
        w_kernel,
        in_specs=[SMEM, VMEM, VMEM],
        out_specs=[VMEM] * (2 + SWAPS),
        out_shape=[
            jax.ShapeDtypeStruct((NY, K, width), F32),
            jax.ShapeDtypeStruct((NY, K, width), F32),
        ]
        + [jax.ShapeDtypeStruct((NY // SWAPS, K, width), BF16)] * SWAPS,
        compiler_params=room(20),
        name="sketch_rows",
    )(scalar(core), sampled, matrix)
    return own, low, high


def fold_kernel(a_ref, *refs):
    high_ref, rest_ref = refs[-2:]
    per = NY // SWAPS
    for y in range(NY):
        w = a_ref[y] + refs[y // per][y % per].astype(F32)
        high = w.astype(BF16)
        high_ref[y] = high
        rest_ref[y] = w - high.astype(F32)


def fold(a, parts):
    return pl.pallas_call(
        fold_kernel,
        in_specs=[VMEM] * (1 + SWAPS),
        out_specs=[VMEM, VMEM],
        out_shape=[jax.ShapeDtypeStruct(a.shape, BF16), jax.ShapeDtypeStruct(a.shape, F32)],
        compiler_params=room(8),
        name="fold",
    )(a, *parts)


def finish_kernel(inv_ref, *refs):
    out_ref = refs[-1]
    terms = [ref[k].astype(F32) for ref in refs[:-1] for k in range(NY)]
    while len(terms) > 1:
        terms = [terms[i] + terms[i + 1] for i in range(0, len(terms), 2)]
    piece = jnp.dot(inv_ref[...], terms[0], precision=HIGH, preferred_element_type=F32).astype(BF16)
    for k in range(NY):
        out_ref[k] = piece


def finish(inverse, *parts):
    return pl.pallas_call(
        finish_kernel,
        in_specs=[VMEM] * (1 + len(parts)),
        out_specs=VMEM,
        out_shape=jax.ShapeDtypeStruct(parts[0].shape, BF16),
        compiler_params=room(8),
        name="finish",
    )(inverse, *parts)


def place_kernel(core_ref, own_ref, other_ref, out_ref, sems):
    width = own_ref.shape[2]
    core = core_ref[0]
    copies = []
    for i, (half, ref) in enumerate(((core, own_ref), (1 - core, other_ref))):
        for y in range(NY):
            at = pl.multiple_of((half * NY + y) * width, width)
            copies.append(
                pltpu.make_async_copy(ref.at[y], out_ref.at[:, pl.ds(at, width)], sems.at[i, y])
            )
    for copy in copies:
        copy.start()
    for copy in copies:
        copy.wait()


def place(own, other, core):
    anywhere = pl.BlockSpec(memory_space=pl.ANY)
    return pl.pallas_call(
        place_kernel,
        in_specs=[SMEM, anywhere, anywhere],
        out_specs=HBM,
        out_shape=jax.ShapeDtypeStruct((K, NROW * own.shape[2]), BF16),
        scratch_shapes=[pltpu.SemaphoreType.DMA((2, NY))],
        compiler_params=room(4),
        name="place",
    )(scalar(core), own, other)


SWAP = [(i, i ^ 1) for i in range(NROW)]
Y_GROUPS = [[2 * k + core for k in range(NY)] for core in range(2)]


def over_y(blocks):
    return lax.all_to_all(blocks, "row", 0, 0, axis_index_groups=Y_GROUPS)


def local(matrix, omega):
    core = lax.axis_index("row") % 2
    x = lax.axis_index("col") // NZ
    rows = matrix.shape[0]

    partial_value = sketch(matrix, omega)
    parts = lax.all_to_all(partial_value.reshape(NCOL, rows // NCOL, K), "col", 0, 0)
    sampled = lax.all_to_all(share(parts, NCOL), "col", 0, 0).reshape(rows, K)

    strips = gram_strips(sampled, x)
    held, strips = lax.optimization_barrier((sampled, strips))
    strips = share(lax.all_to_all(strips, "row", 0, 0), 1)
    own, low, other = sketch_rows(held, matrix, core)
    high, rest = fold(own, [lax.ppermute(part, "row", SWAP) for part in other])
    parts = over_y(high)
    strips = [strips] + [
        lax.ppermute(strips, "col", [(i, i ^ (j * NZ)) for i in range(NCOL)])
        for j in range(1, STRIPS)
    ]
    inverse, growth = chol_inv(strips, x)

    def with_residuals():
        return finish(inverse, parts, over_y(rest + lax.ppermute(low, "row", SWAP)))

    pieces = lax.cond(
        growth[0, 0] <= 2.0 * K, lambda: finish(inverse, parts), with_residuals
    )
    pieces = over_y(pieces)
    basis = lax.dot_general(sampled, inverse, (((1,), (1,)), ((), ())), precision=HIGH).astype(BF16)
    return basis, place(pieces, lax.ppermute(pieces, "row", SWAP), core)


def solution(mesh):
    return jax.shard_map(
        local,
        mesh=mesh,
        in_specs=(P("row", "col"), P("col", None)),
        out_specs=(P("row", None), P(None, "col")),
        check_vma=False,
    )
```
